32 devices in a mesh: hid: 8 (over y, x, core), wid: 4 (over z).
Axes of the slice: x: 2, y: 2, z: 4, core: 2. Of those that a mesh axis runs over, the one named last changes fastest.
Arguments:
- tokens: bfloat16 [512, 8192], P('hid', 'wid'), may hold values from -6 to 6
- out_grad: bfloat16 [512, 8192], P('hid', 'wid'), may hold values from -6 to 6
- gate_weight: bfloat16 [8192, 28672], P('wid', 'hid'), may hold values from -0.0625 to 0.0625
- up_weight: bfloat16 [8192, 28672], P('wid', 'hid'), may hold values from -0.0625 to 0.0625
- down_weight: bfloat16 [28672, 8192], P('hid', 'wid'), may hold values from -0.03125 to 0.03125
- cap_codes: int32 [28672], P('hid'), may hold values from 256 to 2048
Outputs:
- input_grad: bfloat16 [512, 8192], P('hid', 'wid')
- gate_grad: bfloat16 [8192, 28672], P('wid', 'hid')
- up_grad: bfloat16 [8192, 28672], P('wid', 'hid')
- down_grad: bfloat16 [28672, 8192], P('hid', 'wid')
The draws below stay inside these ranges and needn't reach their ends.
Inputs may be any that keep to these rules, and one draw needn't show every extreme that they name: `cap_codes`: each hidden unit's cap is its code divided by 512.
All inputs are finite; a program needn't handle non-finite values.
Results may differ from the reference program's by a relative error of at most 0.005.
Values may be sent and summed in bfloat16 or wider, within the bound.
No kernel may reach another device: no remote copies, remote signals or barrier semaphores. Data moves between devices by JAX's collectives and lax.ppermute only.
A program may use at most 192 MiB of HBM per device.

```python
import jax
import jax.numpy as jnp

D = 8192
FF = 28672
TOKENS = 512


def place_ends(values, rng, least, largest):
    index_at = [jax.random.randint(jax.random.fold_in(rng, axis), (), 0, length) for axis, length in enumerate(values.shape)]
    main_axis = values.shape.index(max(values.shape))
    neighbour = index_at[:main_axis] + [(index_at[main_axis] + 1) % values.shape[main_axis]] + index_at[main_axis + 1:]
    return values.at[tuple(index_at)].set(least).at[tuple(neighbour)].set(largest)


def steps_of(key, extent, pieces, low, high):
    def one(axis_at, blocks):
        steps = jax.random.uniform(jax.random.fold_in(jax.random.fold_in(key, 6), axis_at), (blocks,), jnp.float32, low / len(pieces), high / len(pieces))
        return jnp.repeat(jnp.exp(steps), extent[axis_at] // blocks).reshape((-1,) + (1,) * (len(extent) - axis_at - 1))

    level = one(*pieces[0])
    for cut in pieces[1:]:
        level = level * one(*cut)
    return level


def bell_draw(stream_key, dims, deviation, limit, cuts=(), dtype=jnp.bfloat16):
    drawn = deviation * jax.random.normal(stream_key, dims, jnp.float32)
    if cuts:
        drawn = drawn * steps_of(stream_key, dims, cuts, -0.22, 0.18)
    return jnp.clip(drawn, -limit, limit).astype(dtype)


def setup_inputs(seed: int = 0) -> dict:
    seeds = jax.random.split(jax.random.key(seed), 7)
    tokens = bell_draw(seeds[0], (TOKENS, D), 1.0, 6.0, ((0, 8), (1, 4)))
    out_grad = bell_draw(seeds[1], (TOKENS, D), 1.0, 6.0, ((0, 8), (1, 4)))
    gate_weight = bell_draw(seeds[2], (D, FF), D ** -0.5, 0.0625, ((0, 4), (1, 8)))
    up_weight = bell_draw(seeds[3], (D, FF), D ** -0.5, 0.0625, ((0, 4), (1, 8)))
    down_weight = bell_draw(seeds[4], (FF, D), FF ** -0.5, 0.03125, ((0, 8), (1, 4)))
    cap_codes = place_ends(jax.random.randint(seeds[5], (FF,), 256, 2049), jax.random.fold_in(seeds[5], 1), 256, 2048).astype(jnp.int32)
    return dict(tokens=tokens, out_grad=out_grad, gate_weight=gate_weight, up_weight=up_weight, down_weight=down_weight, cap_codes=cap_codes)


def reference(tokens, out_grad, gate_weight, up_weight, down_weight, cap_codes):
    gate = jnp.dot(tokens, gate_weight, preferred_element_type=jnp.float32)
    up = jnp.dot(tokens, up_weight, preferred_element_type=jnp.float32)
    cap_vals = cap_codes.astype(jnp.float32) * (1.0 / 512.0)
    sigmoid_gate = jax.nn.sigmoid(gate)
    active = gate * sigmoid_gate
    squash = jnp.tanh(active * up / cap_vals[None, :])
    capped = (cap_vals[None, :] * squash).astype(jnp.bfloat16)
    cap_grad = jnp.dot(out_grad, down_weight.T, preferred_element_type=jnp.float32)
    hidden_grad = cap_grad * (1.0 - squash * squash)
    gate_delta = (hidden_grad * up * sigmoid_gate * (1.0 + gate * (1.0 - sigmoid_gate))).astype(jnp.bfloat16)
    up_delta = (hidden_grad * active).astype(jnp.bfloat16)
    input_grad = (jnp.dot(gate_delta, gate_weight.T, preferred_element_type=jnp.float32)
                  + jnp.dot(up_delta, up_weight.T, preferred_element_type=jnp.float32)).astype(jnp.bfloat16)
    gate_grad = jnp.dot(tokens.T, gate_delta, preferred_element_type=jnp.float32).astype(jnp.bfloat16)
    up_grad = jnp.dot(tokens.T, up_delta, preferred_element_type=jnp.float32).astype(jnp.bfloat16)
    down_grad = jnp.dot(capped.T, out_grad, preferred_element_type=jnp.float32).astype(jnp.bfloat16)
    return (input_grad, gate_grad, up_grad, down_grad)
```

```python
import functools

import jax
import jax.numpy as jnp
from jax import lax
from jax.experimental import pallas as pl
from jax.experimental.pallas import tpu as pltpu
from jax.sharding import PartitionSpec as P

MIB = 1024 * 1024
VMEM = {"front": 32, "hidden": 48, "inw": 40, "in": 48, "w": 40}
SLABS = 2
BLOCK = 256
LOOK = 3
BACK = 1
JOINT = False
EARLY = False
AHEAD = 5
UNIT = 512
LAST = 1024
ODD = -2
WEIGH = {"front": 1e-05, "hidden": 1e-05, "inw": 1e-05, "in": 1e-05, "w": 1e-05}


def tie(value, *after):
    return lax.optimization_barrier((value, *after))[0]


def dot_last(left, right):
    return lax.dot_general(left, right, (((1,), (1,)), ((), ())), preferred_element_type=jnp.float32)


def dot_plain(left, right):
    return lax.dot_general(left, right, (((1,), (0,)), ((), ())), preferred_element_type=jnp.float32)


def call(kernel, name, grid, in_specs, out_specs, out_shape, args, aliases=None, scratch=(), flops=0, moved=0):
    return pl.pallas_call(
        kernel,
        grid=(grid,),
        in_specs=in_specs,
        out_specs=out_specs,
        out_shape=out_shape,
        scratch_shapes=list(scratch),
        input_output_aliases=aliases or {},
        compiler_params=pltpu.CompilerParams(vmem_limit_bytes=VMEM[name] * MIB),
        cost_estimate=pl.CostEstimate(flops=int(flops * WEIGH[name]), bytes_accessed=int(moved * WEIGH[name]), transcendentals=0),
        name=name,
    )(*args)


def pick_block(*extents):
    return next(b for b in (256, 384, 128) if all(e % b == 0 for e in extents))


def once(shape, *index):
    return pl.BlockSpec(shape, lambda j: index or (0,) * len(shape), pipeline_mode=pl.Buffered(1))


def within(shape, at, steps, skip=0):
    return pl.BlockSpec(shape, lambda j: (0, 0, jnp.clip(j - at, 0, steps - 1) + skip))


def front_kernel(panels, pieces, bounds, *refs):
    j = pl.program_id(0)
    given, parts = refs[:panels], refs[panels:panels + pieces]
    gate_w, up_w, down_w = refs[panels + pieces:panels + pieces + 3]
    outs = refs[panels + pieces + 3:]
    if pieces:
        tok, grad = outs[:2]
        outs = outs[2:]
        size = parts[0].shape[1]

        @pl.when(j == 0)
        def _():
            at = 0
            if panels:
                at = given[0].shape[0]
                tok[:at, :] = given[0][...]
                grad[:at, :] = given[1][...]
            for i, part in enumerate(parts):
                tok[at + i * size:at + (i + 1) * size, :] = part[0]
                grad[at + i * size:at + (i + 1) * size, :] = part[1]
    else:
        tok, grad = given

    def fill(sums, sent):
        for k in range(3):
            value = (dot_plain(tok[...], gate_w[...]), dot_plain(tok[...], up_w[...]), dot_last(grad[...], down_w[...]))[k]
            sums[k] = value
            sent[k] = value.astype(sent.dtype)

    for u, (low, high) in enumerate(bounds):
        if len(bounds) == 1:
            fill(outs[0], outs[1])
        else:
            pl.when((j >= low) & (j < high))(functools.partial(fill, outs[2 * u], outs[2 * u + 1]))


def front(panel, pieces, part, rows, gate_w, up_w, down_w, spans):
    feats = gate_w.shape[0]
    block = pick_block(*(e for span in spans for e in span))
    first = spans[0][0] // block
    whole = sum(w for _, w in spans)
    cols = pl.BlockSpec((feats, block), lambda j: (0, first + j))
    args = [*panel, *pieces]
    in_specs = [once((rows, feats) if not pieces else p.shape, *((part, 0) if not pieces else ())) for p in panel]
    in_specs += [once(p.shape) for p in pieces]
    out_specs, out_shape, bounds = [], [], []
    if pieces:
        out_specs += [pl.BlockSpec((rows, feats), lambda j: (0, 0))] * 2
        out_shape += [jax.ShapeDtypeStruct((rows, feats), jnp.bfloat16)] * 2
    at = 0
    for _, width in spans:
        steps = width // block
        bounds.append((at, at + steps))
        out_specs += [within((3, rows, block), at, steps)] * 2
        out_shape += [jax.ShapeDtypeStruct((3, rows, width), d) for d in (jnp.float32, jnp.bfloat16)]
        at += steps
    outs = call(
        functools.partial(front_kernel, len(panel), len(pieces), tuple(bounds)),
        "front",
        at,
        in_specs + [cols, cols, pl.BlockSpec((block, feats), lambda j: (first + j, 0))],
        out_specs,
        out_shape,
        [*args, gate_w, up_w, down_w],
        flops=6 * rows * feats * whole,
        moved=6 * feats * whole + 4 * rows * feats + 18 * rows * whole,
    )
    return (outs[:2], outs[2:]) if pieces else (panel, outs)


def next_kernel(sums, inward, out):
    for k in range(3):
        out[k] = (sums[k] + inward[k].astype(jnp.float32)).astype(out.dtype)


def hidden_kernel(both, sums, inward, across, codes, *refs):
    if both:
        next_kernel(*refs[:2], refs[3])
        out = refs[2]
    else:
        out = refs[0]
    cap = codes[...].astype(jnp.float32) * (1.0 / 512.0)
    gate, up, cap_grad = (
        sums[k] + (inward[k].astype(jnp.float32) + across[k].astype(jnp.float32)) for k in range(3)
    )
    sig = 1.0 / (1.0 + jnp.exp(-gate))
    act = gate * sig
    squash = jnp.tanh(act * up * (1.0 / cap))
    hid_grad = cap_grad * (1.0 - squash * squash)
    out[0] = (cap * squash).astype(out.dtype)
    out[1] = (hid_grad * up * sig * (1.0 + gate * (1.0 - sig))).astype(out.dtype)
    out[2] = (hid_grad * act).astype(out.dtype)


def hidden(sums, inward, across, codes, start, ahead=()):
    _, rows, width = sums.shape
    block = pick_block(start, width)
    first = start // block
    wide = width // block
    tall = 256 if rows % 256 == 0 else rows
    spec = pl.BlockSpec((3, tall, block), lambda j: (0, j // wide, j % wide))
    outs = 2 if ahead else 1
    made = call(
        functools.partial(hidden_kernel, bool(ahead)),
        "hidden",
        wide * (rows // tall),
        [spec, spec, spec, pl.BlockSpec((1, block), lambda j: (0, first + j % wide))] + [spec] * len(ahead),
        [spec] * outs,
        [jax.ShapeDtypeStruct((3, rows, width), jnp.bfloat16)] * outs,
        [sums, inward, across, codes, *ahead],
        flops=60 * rows * width,
        moved=30 * rows * width,
    )
    return made if ahead else made[0]


def back_kernel(layout, befores, outs_in, do_w, *refs):
    refs = list(refs)
    take = lambda n: [refs.pop(0) for _ in range(n)]
    (inner,) = take(1)
    segments = [(low, high, [take(2) for _ in range(parts)]) for low, high, parts in layout]
    gate_w, up_w = take(2) if outs_in else (None, None)
    before = take(befores)
    tok_t, grad = take(2) if do_w else (None, None)
    if do_w == 2:
        take(3)
    ends = take(outs_in)
    grads = take(3) if do_w else None
    j = pl.program_id(0)
    keep = inner[0] > 0
    if outs_in:
        total = refs[0] if refs else ends[0]

        @pl.when(j == 0)
        def _():
            at = 0
            for b in before:
                total[at:at + b.shape[0], :] = b[...]
                at += b.shape[0]
            if at < total.shape[0]:
                total[at:, :] = jnp.zeros((total.shape[0] - at, total.shape[1]), total.dtype)

    def work(parts):
        deltas = []
        for k in range(3):
            rows = [jnp.where(keep, own[k], got[k]) for own, got in parts]
            deltas.append(rows[0] if len(rows) == 1 else jnp.concatenate(rows, axis=0))
        capped, gate_d, up_d = deltas
        if outs_in:
            total[...] += dot_last(gate_d, gate_w[...]) + dot_last(up_d, up_w[...])
        if do_w:
            gate_g, up_g, down_g = grads
            gate_g[...] = dot_plain(tok_t[...], gate_d).astype(gate_g.dtype)
            up_g[...] = dot_plain(tok_t[...], up_d).astype(up_g.dtype)
            down_g[...] = dot_plain(capped.T, grad[...]).astype(down_g.dtype)

    for low, high, parts in segments:
        if len(segments) == 1:
            work(parts)
        else:
            pl.when((j >= low) & (j < high))(functools.partial(work, parts))

    if outs_in > 1:

        @pl.when(j == pl.num_programs(0) - 1)
        def _():
            at = 0
            for end in ends:
                end[...] = total[at:at + end.shape[0], :]
                at += end.shape[0]


def back(inner, segments, gate_w, up_w, before=(), cuts=(), turned=None, old=None):
    feats, columns = gate_w.shape
    block = pick_block(*(e for s in segments for e in (s[0], s[1], s[3])))
    first = segments[0][0] // block
    rows = sum(own.shape[1] for own, _ in segments[0][2])
    cols = pl.BlockSpec((feats, block), lambda j: (0, first + j))
    in_specs, args, layout, aliases = [pl.BlockSpec(memory_space=pltpu.SMEM)], [inner], [], {}
    at = 0
    for _, width, parts, skip in segments:
        steps = width // block
        layout.append((at, at + steps, len(parts)))
        for own, got in parts:
            in_specs += [within((3, own.shape[1], block), at, steps, skip // block)] * 2
            args += [own, got]
        at += steps
    out_specs, out_shape, scratch = [], [], []
    if cuts:
        in_specs += [cols, cols] + [once(b.shape) for b in before]
        args += [gate_w, up_w, *before]
        out_specs += [pl.BlockSpec((c, feats), lambda j: (0, 0)) for c in cuts]
        out_shape += [jax.ShapeDtypeStruct((c, feats), jnp.float32) for c in cuts]
        if len(cuts) > 1:
            scratch = [pltpu.VMEM((rows, feats), jnp.float32)]
    if turned is not None:
        in_specs += [once(a.shape) for a in turned]
        args += [*turned]
        for k, a in enumerate(old or ()):
            in_specs += [pl.BlockSpec(memory_space=pl.ANY)]
            args += [a]
            aliases[len(args) - 1] = len(cuts) + k
        out_specs += [cols, cols, pl.BlockSpec((block, feats), lambda j: (first + j, 0))]
        out_shape += [jax.ShapeDtypeStruct(s, jnp.bfloat16) for s in ((feats, columns), (feats, columns), (columns, feats))]
    do_w = 0 if turned is None else (2 if old else 1)
    width = at * block
    outs = call(
        functools.partial(back_kernel, tuple(layout), len(before), len(cuts), do_w),
        ("in" if cuts else "") + ("w" if do_w else ""),
        at,
        in_specs,
        out_specs,
        out_shape,
        args,
        aliases,
        scratch,
        flops=((4 if cuts else 0) + (6 if do_w else 0)) * rows * feats * width,
        moved=((4 if cuts else 0) + (6 if do_w else 0)) * feats * width + 8 * rows * feats + 12 * rows * width,
    )
    return outs[:len(cuts)], outs[len(cuts):]


def per_device(n_hid, n_wid, tokens, out_grad, gate_weight, up_weight, down_weight, cap_codes):
    half = n_wid // 2
    chips = n_hid // 2
    columns = gate_weight.shape[1]
    piece = tokens.shape[0] // SLABS
    slab_rows = n_hid * piece
    shared = 4 * BLOCK
    mats = (gate_weight, up_weight, down_weight)

    def across_hid(x, flip):
        return lax.ppermute(x, "hid", [(i, i ^ flip) for i in range(n_hid)])

    def gather(slab, mark):
        rows = slice(slab * piece, (slab + 1) * piece)
        own = jnp.stack([tokens[rows], out_grad[rows]])
        if mark is not None:
            own = tie(own, mark)
        even = [own] + [across_hid(own, 2 * m) for m in range(1, chips)]
        if mark is None:
            return even + [across_hid(part, 1) for part in even]
        both = jnp.concatenate(even, axis=1)
        return [both, across_hid(both, 1)]

    def scatter(low, high):
        kept = low + across_hid(high, 1)
        kept = kept.reshape(chips, -1, kept.shape[1])
        small = kept.astype(jnp.bfloat16)
        result = kept[0]
        for m in range(1, chips):
            result = result + across_hid(small[m], 2 * m).astype(jnp.float32)
        return result.astype(jnp.bfloat16)

    codes = cap_codes.reshape(1, -1)
    place = lax.axis_index("wid")
    inner = ((place == half - 1) | (place == half)).astype(jnp.int32).reshape(1)

    units = [(0, shared)] + [(c, min(UNIT, columns - c)) for c in range(shared, columns, UNIT)] + [(0, shared)]
    units[ODD], units[-2] = units[-2], units[ODD]
    count = len(units)
    final = count - 1
    full = list(range(1, final))
    groups = [[u] for u in full]
    fronts = [[u] for u in range(count)]

    sums, message, inward, across, made, got = ({} for _ in range(6))
    mark = None
    panel = None
    turned = None

    def run_front(u):
        nonlocal mark, panel, turned
        if u in message:
            return
        members = next(b for b in fronts if u in b)
        spans = [units[m] for m in members]
        if u == 0:
            panel, outs = front((), gather(0, None), 0, slab_rows, *mats, spans)
        elif u == 1:
            pieces = [tie(p, mark) for p in later]
            panel, outs = front(panel, pieces, 0, SLABS * slab_rows, *mats, spans)
            turned = (panel[0].T, panel[1])
        else:
            given = (tie(panel[0], mark), panel[1])
            if u == final:
                _, outs = front(given, (), 1, slab_rows, *mats, spans)
            else:
                _, outs = front(given, (), 0, SLABS * slab_rows, *mats, spans)
        for i, m in enumerate(members):
            sums[m], message[m] = outs[2 * i], outs[2 * i + 1]
        mark = message[members[-1]]

    def run_inward(u):
        message[u] = tie(message[u], mark)
        inward[u] = jnp.zeros_like(message[u])
        for k in range(half - 1):
            if k:
                message[u] = (sums[u] + inward[u].astype(jnp.float32)).astype(jnp.bfloat16)
            inward[u] = lax.ppermute(message[u], "wid", [(k, k + 1), (n_wid - 1 - k, n_wid - 2 - k)])

    def send_across(u):
        across[u] = lax.ppermute(message[u], "wid", [(half - 1, half), (half, half - 1)])

    def run_middle(u):
        nonlocal mark
        arrived = tie(inward[u], mark)
        mark = message[u] = (sums[u] + arrived.astype(jnp.float32)).astype(jnp.bfloat16)
        send_across(u)

    def run_hidden(u, joint=False):
        nonlocal mark
        arrived = tie(across[u], mark)
        if joint:
            made[u], message[u + 1] = hidden(sums[u], inward[u], arrived, codes, units[u][0], (sums[u + 1], inward[u + 1]))
            mark = made[u]
            send_across(u + 1)
        else:
            mark = made[u] = hidden(sums[u], inward[u], arrived, codes, units[u][0])
        last = made[u]
        for k in range(half - 1):
            last = lax.ppermute(last, "wid", [(half - 1 - k, half - 2 - k), (half + k, half + k + 1)])
            got[u] = last if k == 0 else got[u] + last

    def pair(u):
        return made[u], got.get(u, made[u])

    total, grads, results = [], None, []
    rows = SLABS * slab_rows
    quarter = slab_rows // 2

    def run_back(members, cuts, weights, after=()):
        nonlocal mark, total, grads
        segments = [(*units[m], [pair(m)], 0) for m in members]
        own, arrived = segments[0][2][0]
        segments[0][2][0] = (own, tie(arrived, mark, *after))
        total, new = back(inner, segments, *mats[:2], before=tuple(total), cuts=cuts, turned=turned if weights else None, old=grads)
        mark = total[-1]
        if weights:
            grads = new

    def run_weights(segments):
        nonlocal mark, grads
        own, arrived = segments[0][2][0]
        segments[0][2][0] = (own, tie(arrived, mark))
        _, grads = back(inner, segments, *mats[:2], turned=turned, old=grads)
        mark = grads[0]

    later = None
    for t in range(-LOOK, count + 1):
        joint = JOINT and t > 0 and t + 2 < count and sums[t].shape == sums[t + 1].shape
        if 0 <= t + 1 < count and not joint:
            run_middle(t + 1)
        if 0 <= t < count:
            run_hidden(t, joint)
        if t + LOOK < count:
            run_front(t + LOOK)
            run_inward(t + LOOK)
            if t + LOOK == 0:
                later = gather(1, mark)
        if t > -LOOK:
            for u in range(t + LOOK + 1, min(t + AHEAD + 1, count)):
                run_front(u)
        if t == BACK:
            run_back([0], (slab_rows,), False)
        for g in groups[:-1]:
            if t == g[-1] + BACK:
                run_back(g, (rows,), True)
        if t == groups[-1][-1] + 1:
            run_back(groups[-1], (quarter, quarter, slab_rows), False)
            results.append(scatter(*total[:2]))
            total = total[2:]
        if t == 0:
            mark = tie(mark, turned[0])
        if t == count:
            run_weights([(*units[m], [pair(m)], 0) for m in groups[-1]])
            run_back([final], (quarter, quarter), False, results[:1] if EARLY else ())
            results.append(scatter(*total))
    for part in range(0, shared, LAST):
        run_weights([(units[0][0] + part, LAST, [pair(0), pair(final)], part)])

    return (jnp.concatenate(results, axis=0), *grads)


def solution(mesh):
    return jax.shard_map(
        functools.partial(per_device, mesh.shape["hid"], mesh.shape["wid"]),
        mesh=mesh,
        in_specs=(
            P("hid", "wid"),
            P("hid", "wid"),
            P("wid", "hid"),
            P("wid", "hid"),
            P("hid", "wid"),
            P("hid"),
        ),
        out_specs=(P("hid", "wid"), P("wid", "hid"), P("wid", "hid"), P("hid", "wid")),
        check_vma=False,
    )
```

```python
import functools

import jax
import jax.numpy as jnp
from jax import lax
from jax.experimental import pallas as pl
from jax.experimental.pallas import tpu as pltpu
from jax.sharding import PartitionSpec as P

MIB = 1024 * 1024
VMEM = {"front": 32, "hidden": 48, "inw": 40, "in": 48, "w": 40}
SLABS = 2
BLOCK = 256
LOOK = 3
HELD = 1
TURN = 1
BACK = 1
JOINT = False
AHEAD = 5
UNIT = 512
ODD = -2
WEIGH = {"front": 1e-05, "hidden": 1e-05, "inw": 1e-05, "in": 1e-05, "w": 1e-05}


def tie(value, *after):
    return lax.optimization_barrier((value, *after))[0]


def dot_last(left, right):
    return lax.dot_general(left, right, (((1,), (1,)), ((), ())), preferred_element_type=jnp.float32)


def dot_plain(left, right):
    return lax.dot_general(left, right, (((1,), (0,)), ((), ())), preferred_element_type=jnp.float32)


def call(kernel, name, grid, in_specs, out_specs, out_shape, args, aliases=None, scratch=(), flops=0, moved=0):
    return pl.pallas_call(
        kernel,
        grid=(grid,),
        in_specs=in_specs,
        out_specs=out_specs,
        out_shape=out_shape,
        scratch_shapes=list(scratch),
        input_output_aliases=aliases or {},
        compiler_params=pltpu.CompilerParams(vmem_limit_bytes=VMEM[name] * MIB),
        cost_estimate=pl.CostEstimate(flops=int(flops * WEIGH[name]), bytes_accessed=int(moved * WEIGH[name]), transcendentals=0),
        name=name,
    )(*args)


def pick_block(*extents):
    return next(b for b in (256, 384, 128) if all(e % b == 0 for e in extents))


def once(shape, *index):
    return pl.BlockSpec(shape, lambda j: index or (0,) * len(shape), pipeline_mode=pl.Buffered(1))


def within(shape, at, steps, skip=0):
    return pl.BlockSpec(shape, lambda j: (0, 0, jnp.clip(j - at, 0, steps - 1) + skip))


def front_kernel(panels, pieces, bounds, *refs):
    j = pl.program_id(0)
    given, parts = refs[:panels], refs[panels:panels + pieces]
    gate_w, up_w, down_w = refs[panels + pieces:panels + pieces + 3]
    outs = refs[panels + pieces + 3:]
    if pieces:
        tok, grad = outs[:2]
        outs = outs[2:]
        size = parts[0].shape[1]

        @pl.when(j == 0)
        def _():
            at = 0
            if panels:
                at = given[0].shape[0]
                tok[:at, :] = given[0][...]
                grad[:at, :] = given[1][...]
            for i, part in enumerate(parts):
                tok[at + i * size:at + (i + 1) * size, :] = part[0]
                grad[at + i * size:at + (i + 1) * size, :] = part[1]
    else:
        tok, grad = given

    def fill(sums, sent):
        for k in range(3):
            value = (dot_plain(tok[...], gate_w[...]), dot_plain(tok[...], up_w[...]), dot_last(grad[...], down_w[...]))[k]
            sums[k] = value
            sent[k] = value.astype(sent.dtype)

    for u, (low, high) in enumerate(bounds):
        if len(bounds) == 1:
            fill(outs[0], outs[1])
        else:
            pl.when((j >= low) & (j < high))(functools.partial(fill, outs[2 * u], outs[2 * u + 1]))


def front(panel, pieces, part, rows, gate_w, up_w, down_w, spans):
    feats = gate_w.shape[0]
    block = pick_block(*(e for span in spans for e in span))
    first = spans[0][0] // block
    whole = sum(w for _, w in spans)
    cols = pl.BlockSpec((feats, block), lambda j: (0, first + j))
    args = [*panel, *pieces]
    in_specs = [once((rows, feats) if not pieces else p.shape, *((part, 0) if not pieces else ())) for p in panel]
    in_specs += [once(p.shape) for p in pieces]
    out_specs, out_shape, bounds = [], [], []
    if pieces:
        out_specs += [pl.BlockSpec((rows, feats), lambda j: (0, 0))] * 2
        out_shape += [jax.ShapeDtypeStruct((rows, feats), jnp.bfloat16)] * 2
    at = 0
    for _, width in spans:
        steps = width // block
        bounds.append((at, at + steps))
        out_specs += [within((3, rows, block), at, steps)] * 2
        out_shape += [jax.ShapeDtypeStruct((3, rows, width), d) for d in (jnp.float32, jnp.bfloat16)]
        at += steps
    outs = call(
        functools.partial(front_kernel, len(panel), len(pieces), tuple(bounds)),
        "front",
        at,
        in_specs + [cols, cols, pl.BlockSpec((block, feats), lambda j: (first + j, 0))],
        out_specs,
        out_shape,
        [*args, gate_w, up_w, down_w],
        flops=6 * rows * feats * whole,
        moved=6 * feats * whole + 4 * rows * feats + 18 * rows * whole,
    )
    return (outs[:2], outs[2:]) if pieces else (panel, outs)


def next_kernel(sums, inward, out):
    for k in range(3):
        out[k] = (sums[k] + inward[k].astype(jnp.float32)).astype(out.dtype)


def hidden_kernel(both, sums, inward, across, codes, *refs):
    if both:
        next_kernel(*refs[:2], refs[3])
        out = refs[2]
    else:
        out = refs[0]
    cap = codes[...].astype(jnp.float32) * (1.0 / 512.0)
    gate, up, cap_grad = (
        sums[k] + (inward[k].astype(jnp.float32) + across[k].astype(jnp.float32)) for k in range(3)
    )
    sig = 1.0 / (1.0 + jnp.exp(-gate))
    act = gate * sig
    squash = jnp.tanh(act * up * (1.0 / cap))
    hid_grad = cap_grad * (1.0 - squash * squash)
    out[0] = (cap * squash).astype(out.dtype)
    out[1] = (hid_grad * up * sig * (1.0 + gate * (1.0 - sig))).astype(out.dtype)
    out[2] = (hid_grad * act).astype(out.dtype)


def hidden(sums, inward, across, codes, start, ahead=()):
    _, rows, width = sums.shape
    block = pick_block(start, width)
    first = start // block
    wide = width // block
    tall = 256 if rows % 256 == 0 else rows
    spec = pl.BlockSpec((3, tall, block), lambda j: (0, j // wide, j % wide))
    outs = 2 if ahead else 1
    made = call(
        functools.partial(hidden_kernel, bool(ahead)),
        "hidden",
        wide * (rows // tall),
        [spec, spec, spec, pl.BlockSpec((1, block), lambda j: (0, first + j % wide))] + [spec] * len(ahead),
        [spec] * outs,
        [jax.ShapeDtypeStruct((3, rows, width), jnp.bfloat16)] * outs,
        [sums, inward, across, codes, *ahead],
        flops=60 * rows * width,
        moved=30 * rows * width,
    )
    return made if ahead else made[0]


def back_kernel(layout, befores, outs_in, do_w, *refs):
    refs = list(refs)
    take = lambda n: [refs.pop(0) for _ in range(n)]
    (inner,) = take(1)
    segments = [(low, high, [take(2) for _ in range(parts)]) for low, high, parts in layout]
    gate_w, up_w = take(2) if outs_in else (None, None)
    before = take(befores)
    tok_t, grad = take(2) if do_w else (None, None)
    if do_w == 2:
        take(3)
    ends = take(outs_in)
    grads = take(3) if do_w else None
    j = pl.program_id(0)
    keep = inner[0] > 0
    if outs_in:
        total = refs[0] if refs else ends[0]

        @pl.when(j == 0)
        def _():
            at = 0
            for b in before:
                total[at:at + b.shape[0], :] = b[...]
                at += b.shape[0]
            if at < total.shape[0]:
                total[at:, :] = jnp.zeros((total.shape[0] - at, total.shape[1]), total.dtype)

    def work(parts):
        deltas = []
        for k in range(3):
            rows = [jnp.where(keep, own[k], got[k]) for own, got in parts]
            deltas.append(rows[0] if len(rows) == 1 else jnp.concatenate(rows, axis=0))
        capped, gate_d, up_d = deltas
        if outs_in:
            total[...] += dot_last(gate_d, gate_w[...]) + dot_last(up_d, up_w[...])
        if do_w:
            gate_g, up_g, down_g = grads
            gate_g[...] = dot_plain(tok_t[...], gate_d).astype(gate_g.dtype)
            up_g[...] = dot_plain(tok_t[...], up_d).astype(up_g.dtype)
            down_g[...] = dot_plain(capped.T, grad[...]).astype(down_g.dtype)

    for low, high, parts in segments:
        if len(segments) == 1:
            work(parts)
        else:
            pl.when((j >= low) & (j < high))(functools.partial(work, parts))

    if outs_in > 1:

        @pl.when(j == pl.num_programs(0) - 1)
        def _():
            at = 0
            for end in ends:
                end[...] = total[at:at + end.shape[0], :]
                at += end.shape[0]


def back(inner, segments, gate_w, up_w, before=(), cuts=(), turned=None, old=None):
    feats, columns = gate_w.shape
    block = pick_block(*(e for s in segments for e in (s[0], s[1], s[3])))
    first = segments[0][0] // block
    rows = sum(own.shape[1] for own, _ in segments[0][2])
    cols = pl.BlockSpec((feats, block), lambda j: (0, first + j))
    in_specs, args, layout, aliases = [pl.BlockSpec(memory_space=pltpu.SMEM)], [inner], [], {}
    at = 0
    for _, width, parts, skip in segments:
        steps = width // block
        layout.append((at, at + steps, len(parts)))
        for own, got in parts:
            in_specs += [within((3, own.shape[1], block), at, steps, skip // block)] * 2
            args += [own, got]
        at += steps
    out_specs, out_shape, scratch = [], [], []
    if cuts:
        in_specs += [cols, cols] + [once(b.shape) for b in before]
        args += [gate_w, up_w, *before]
        out_specs += [pl.BlockSpec((c, feats), lambda j: (0, 0)) for c in cuts]
        out_shape += [jax.ShapeDtypeStruct((c, feats), jnp.float32) for c in cuts]
        if len(cuts) > 1:
            scratch = [pltpu.VMEM((rows, feats), jnp.float32)]
    if turned is not None:
        in_specs += [once(a.shape) for a in turned]
        args += [*turned]
        for k, a in enumerate(old or ()):
            in_specs += [pl.BlockSpec(memory_space=pl.ANY)]
            args += [a]
            aliases[len(args) - 1] = len(cuts) + k
        out_specs += [cols, cols, pl.BlockSpec((block, feats), lambda j: (first + j, 0))]
        out_shape += [jax.ShapeDtypeStruct(s, jnp.bfloat16) for s in ((feats, columns), (feats, columns), (columns, feats))]
    do_w = 0 if turned is None else (2 if old else 1)
    width = at * block
    outs = call(
        functools.partial(back_kernel, tuple(layout), len(before), len(cuts), do_w),
        ("in" if cuts else "") + ("w" if do_w else ""),
        at,
        in_specs,
        out_specs,
        out_shape,
        args,
        aliases,
        scratch,
        flops=((4 if cuts else 0) + (6 if do_w else 0)) * rows * feats * width,
        moved=((4 if cuts else 0) + (6 if do_w else 0)) * feats * width + 8 * rows * feats + 12 * rows * width,
    )
    return outs[:len(cuts)], outs[len(cuts):]


def per_device(n_hid, n_wid, tokens, out_grad, gate_weight, up_weight, down_weight, cap_codes):
    half = n_wid // 2
    chips = n_hid // 2
    columns = gate_weight.shape[1]
    piece = tokens.shape[0] // SLABS
    slab_rows = n_hid * piece
    shared = 4 * BLOCK
    mats = (gate_weight, up_weight, down_weight)

    def across_hid(x, flip):
        return lax.ppermute(x, "hid", [(i, i ^ flip) for i in range(n_hid)])

    def gather(slab, mark):
        rows = slice(slab * piece, (slab + 1) * piece)
        own = jnp.stack([tokens[rows], out_grad[rows]])
        if mark is not None:
            own = tie(own, mark)
        even = [own] + [across_hid(own, 2 * m) for m in range(1, chips)]
        if mark is None:
            return even + [across_hid(part, 1) for part in even]
        both = jnp.concatenate(even, axis=1)
        return [both, across_hid(both, 1)]

    def fold(low, high):
        return (low + across_hid(high, 1)).reshape(chips, -1, low.shape[1])

    def scatter(parts):
        small = jnp.concatenate([p.astype(jnp.bfloat16) for p in parts], axis=1)
        result = jnp.concatenate([p[0] for p in parts], axis=0)
        for m in range(1, chips):
            result = result + across_hid(small[m], 2 * m).astype(jnp.float32)
        return result.astype(jnp.bfloat16)

    codes = cap_codes.reshape(1, -1)
    place = lax.axis_index("wid")
    inner = ((place == half - 1) | (place == half)).astype(jnp.int32).reshape(1)

    units = [(0, shared)] + [(c, min(UNIT, columns - c)) for c in range(shared, columns, UNIT)] + [(0, shared)]
    units[ODD], units[-2] = units[-2], units[ODD]
    count = len(units)
    final = count - 1
    full = list(range(1, final))
    groups = [[u] for u in full]
    fronts = [[u] for u in range(count)]

    sums, message, inward, across, made, got = ({} for _ in range(6))
    mark = None
    panel = None
    held = None
    turned = None

    def run_front(u):
        nonlocal mark, panel, turned, held
        if u in message:
            return
        members = next(b for b in fronts if u in b)
        spans = [units[m] for m in members]
        if u == 0:
            held = gather(0, None)
            panel, outs = front((), held, 0, slab_rows, *mats, spans)
        elif u == 1:
            pieces = [tie(p, mark) for p in later]
            panel, outs = front(panel, pieces, 0, SLABS * slab_rows, *mats, spans)
            turned = (panel[0].T, panel[1])
        else:
            given = (tie(panel[0], mark), panel[1])
            if u == final:
                _, outs = front(given, (), 1, slab_rows, *mats, spans)
            else:
                _, outs = front(given, (), 0, SLABS * slab_rows, *mats, spans)
        for i, m in enumerate(members):
            sums[m], message[m] = outs[2 * i], outs[2 * i + 1]
        mark = message[members[-1]]

    def run_inward(u):
        message[u] = tie(message[u], mark)
        inward[u] = jnp.zeros_like(message[u])
        for k in range(half - 1):
            if k:
                message[u] = (sums[u] + inward[u].astype(jnp.float32)).astype(jnp.bfloat16)
            inward[u] = lax.ppermute(message[u], "wid", [(k, k + 1), (n_wid - 1 - k, n_wid - 2 - k)])

    def send_across(u):
        across[u] = lax.ppermute(message[u], "wid", [(half - 1, half), (half, half - 1)])

    def run_middle(u):
        nonlocal mark
        arrived = tie(inward[u], mark, *(turned[:1] if u == TURN else ()))
        mark = message[u] = (sums[u] + arrived.astype(jnp.float32)).astype(jnp.bfloat16)
        send_across(u)

    def run_hidden(u, joint=False):
        nonlocal mark
        arrived = tie(across[u], mark)
        if joint:
            made[u], message[u + 1] = hidden(sums[u], inward[u], arrived, codes, units[u][0], (sums[u + 1], inward[u + 1]))
            mark = made[u]
            send_across(u + 1)
        else:
            mark = made[u] = hidden(sums[u], inward[u], arrived, codes, units[u][0])
        last = made[u]
        for k in range(half - 1):
            last = lax.ppermute(last, "wid", [(half - 1 - k, half - 2 - k), (half + k, half + k + 1)])
            got[u] = last if k == 0 else got[u] + last

    def pair(u):
        return made[u], got.get(u, made[u])

    total, grads, folded = [], None, []
    rows = SLABS * slab_rows
    quarter = slab_rows // 2

    def run_back(members, cuts, weights):
        nonlocal mark, total, grads
        segments = [(*units[m], [pair(m)], 0) for m in members]
        own, arrived = segments[0][2][0]
        segments[0][2][0] = (own, tie(arrived, mark))
        total, new = back(inner, segments, *mats[:2], before=tuple(total), cuts=cuts, turned=turned if weights else None, old=grads)
        mark = total[-1]
        if weights:
            grads = new

    def run_weights(segments):
        nonlocal mark, grads
        own, arrived = segments[0][2][0]
        segments[0][2][0] = (own, tie(arrived, mark))
        _, grads = back(inner, segments, *mats[:2], turned=turned, old=grads)
        mark = grads[0]

    later = None
    for t in range(-LOOK, count + 1):
        joint = JOINT and t > 0 and t + 2 < count and sums[t].shape == sums[t + 1].shape
        if 0 <= t + 1 < count and not joint:
            run_middle(t + 1)
        if 0 <= t < count:
            run_hidden(t, joint)
        if t + LOOK < count:
            run_front(t + LOOK)
            run_inward(t + LOOK)
            if t + LOOK == 0:
                later = gather(1, mark if HELD < 0 else held[HELD])
        if t > -LOOK:
            for u in range(t + LOOK + 1, min(t + AHEAD + 1, count)):
                run_front(u)
        if t == BACK:
            run_back([0], (slab_rows,), False)
        for g in groups[:-1]:
            if t == g[-1] + BACK:
                run_back(g, (rows,), True)
        if t == groups[-1][-1] + 1:
            run_back(groups[-1], (quarter, quarter, slab_rows), False)
            folded.append(fold(*total[:2]))
            total = total[2:]
        if t == count:
            run_weights([(*units[m], [pair(m)], 0) for m in groups[-1]])
            run_back([final], (quarter, quarter), False)
            folded.append(fold(*total))
            run_weights([(units[0][0], shared, [pair(0), pair(final)], 0)])

    return (scatter(folded), *grads)


def solution(mesh):
    return jax.shard_map(
        functools.partial(per_device, mesh.shape["hid"], mesh.shape["wid"]),
        mesh=mesh,
        in_specs=(
            P("hid", "wid"),
            P("hid", "wid"),
            P("wid", "hid"),
            P("wid", "hid"),
            P("hid", "wid"),
            P("hid"),
        ),
        out_specs=(P("hid", "wid"), P("wid", "hid"), P("wid", "hid"), P("hid", "wid")),
        check_vma=False,
    )
```

```python
import functools

import jax
import jax.numpy as jnp
from jax import lax
from jax.experimental import pallas as pl
from jax.experimental.pallas import tpu as pltpu
from jax.sharding import PartitionSpec as P

MIB = 1024 * 1024
VMEM = {"front": 32, "hidden": 48, "inw": 40, "in": 48, "w": 40}
SLABS = 2
BLOCK = 256
LOOK = 3
HELD = 1
TURN = 1
BACK = 1
JOINT = False
AHEAD = 5
UNIT = 512
ODD = -2
WEIGH = {"front": 1e-05, "hidden": 1e-05, "inw": 1e-05, "in": 1e-05, "w": 1e-05}


def tie(value, *after):
    return lax.optimization_barrier((value, *after))[0]


def dot_last(left, right):
    return lax.dot_general(left, right, (((1,), (1,)), ((), ())), preferred_element_type=jnp.float32)


def dot_plain(left, right):
    return lax.dot_general(left, right, (((1,), (0,)), ((), ())), preferred_element_type=jnp.float32)


def call(kernel, name, grid, in_specs, out_specs, out_shape, args, aliases=None, scratch=(), flops=0, moved=0):
    return pl.pallas_call(
        kernel,
        grid=(grid,),
        in_specs=in_specs,
        out_specs=out_specs,
        out_shape=out_shape,
        scratch_shapes=list(scratch),
        input_output_aliases=aliases or {},
        compiler_params=pltpu.CompilerParams(vmem_limit_bytes=VMEM[name] * MIB),
        cost_estimate=pl.CostEstimate(flops=int(flops * WEIGH[name]), bytes_accessed=int(moved * WEIGH[name]), transcendentals=0),
        name=name,
    )(*args)


def pick_block(*extents):
    return next(b for b in (256, 384, 128) if all(e % b == 0 for e in extents))


def once(shape, *index):
    return pl.BlockSpec(shape, lambda j: index or (0,) * len(shape), pipeline_mode=pl.Buffered(1))


def within(shape, at, steps, skip=0):
    return pl.BlockSpec(shape, lambda j: (0, 0, jnp.clip(j - at, 0, steps - 1) + skip))


def front_kernel(panels, pieces, inside, bounds, *refs):
    j = pl.program_id(0)
    given, parts = refs[:panels], refs[panels:panels + pieces]
    gate_w, up_w, down_w = refs[panels + pieces:panels + pieces + 3]
    outs = refs[panels + pieces + 3:]
    if pieces:
        tok, grad = outs[-2:] if inside else outs[:2]
        outs = outs[:-2] if inside else outs[2:]
        @pl.when(j == 0)
        def _():
            at = 0
            if panels:
                at = given[0].shape[0]
                tok[:at, :] = given[0][...]
                grad[:at, :] = given[1][...]
            for part in parts:
                size = part.shape[1]
                tok[at:at + size, :] = part[0]
                grad[at:at + size, :] = part[1]
                at += size
    else:
        tok, grad = given

    def fill(sums, sent):
        for k in range(3):
            value = (dot_plain(tok[...], gate_w[...]), dot_plain(tok[...], up_w[...]), dot_last(grad[...], down_w[...]))[k]
            sums[k] = value
            sent[k] = value.astype(sent.dtype)

    for u, (low, high) in enumerate(bounds):
        if len(bounds) == 1:
            fill(outs[0], outs[1])
        else:
            pl.when((j >= low) & (j < high))(functools.partial(fill, outs[2 * u], outs[2 * u + 1]))


def front(panel, pieces, part, rows, gate_w, up_w, down_w, spans, inside=False):
    feats = gate_w.shape[0]
    block = pick_block(*(e for span in spans for e in span))
    first = spans[0][0] // block
    whole = sum(w for _, w in spans)
    cols = pl.BlockSpec((feats, block), lambda j: (0, first + j))
    args = [*panel, *pieces]
    in_specs = [once((rows, feats) if not pieces else p.shape, *((part, 0) if not pieces else ())) for p in panel]
    in_specs += [once(p.shape) for p in pieces]
    out_specs, out_shape, bounds = [], [], []
    if pieces and not inside:
        out_specs += [pl.BlockSpec((rows, feats), lambda j: (0, 0))] * 2
        out_shape += [jax.ShapeDtypeStruct((rows, feats), jnp.bfloat16)] * 2
    at = 0
    for _, width in spans:
        steps = width // block
        bounds.append((at, at + steps))
        out_specs += [within((3, rows, block), at, steps)] * 2
        out_shape += [jax.ShapeDtypeStruct((3, rows, width), d) for d in (jnp.float32, jnp.bfloat16)]
        at += steps
    outs = call(
        functools.partial(front_kernel, len(panel), len(pieces), inside, tuple(bounds)),
        "front",
        at,
        in_specs + [cols, cols, pl.BlockSpec((block, feats), lambda j: (first + j, 0))],
        out_specs,
        out_shape,
        [*args, gate_w, up_w, down_w],
        scratch=[pltpu.VMEM((rows, feats), jnp.bfloat16)] * 2 if inside else (),
        flops=6 * rows * feats * whole,
        moved=6 * feats * whole + 4 * rows * feats + 18 * rows * whole,
    )
    return (outs[:2], outs[2:]) if pieces and not inside else (panel, outs)


def next_kernel(sums, inward, out):
    for k in range(3):
        out[k] = (sums[k] + inward[k].astype(jnp.float32)).astype(out.dtype)


def hidden_kernel(both, sums, inward, across, codes, *refs):
    if both:
        next_kernel(*refs[:2], refs[3])
        out = refs[2]
    else:
        out = refs[0]
    cap = codes[...].astype(jnp.float32) * (1.0 / 512.0)
    gate, up, cap_grad = (
        sums[k] + (inward[k].astype(jnp.float32) + across[k].astype(jnp.float32)) for k in range(3)
    )
    sig = 1.0 / (1.0 + jnp.exp(-gate))
    act = gate * sig
    squash = jnp.tanh(act * up * (1.0 / cap))
    hid_grad = cap_grad * (1.0 - squash * squash)
    out[0] = (cap * squash).astype(out.dtype)
    out[1] = (hid_grad * up * sig * (1.0 + gate * (1.0 - sig))).astype(out.dtype)
    out[2] = (hid_grad * act).astype(out.dtype)


def hidden(sums, inward, across, codes, start, ahead=()):
    _, rows, width = sums.shape
    block = pick_block(start, width)
    first = start // block
    wide = width // block
    tall = 256 if rows % 256 == 0 else rows
    spec = pl.BlockSpec((3, tall, block), lambda j: (0, j // wide, j % wide))
    outs = 2 if ahead else 1
    made = call(
        functools.partial(hidden_kernel, bool(ahead)),
        "hidden",
        wide * (rows // tall),
        [spec, spec, spec, pl.BlockSpec((1, block), lambda j: (0, first + j % wide))] + [spec] * len(ahead),
        [spec] * outs,
        [jax.ShapeDtypeStruct((3, rows, width), jnp.bfloat16)] * outs,
        [sums, inward, across, codes, *ahead],
        flops=60 * rows * width,
        moved=30 * rows * width,
    )
    return made if ahead else made[0]


def back_kernel(layout, befores, outs_in, do_w, *refs):
    refs = list(refs)
    take = lambda n: [refs.pop(0) for _ in range(n)]
    (inner,) = take(1)
    segments = [(low, high, [take(2) for _ in range(parts)]) for low, high, parts in layout]
    gate_w, up_w = take(2) if outs_in else (None, None)
    before = take(befores)
    tok_t, grad = take(2) if do_w else (None, None)
    if do_w == 2:
        take(3)
    ends = take(outs_in)
    grads = take(3) if do_w else None
    j = pl.program_id(0)
    keep = inner[0] > 0
    if outs_in:
        total = refs[0] if refs else ends[0]

        @pl.when(j == 0)
        def _():
            at = 0
            for b in before:
                total[at:at + b.shape[0], :] = b[...]
                at += b.shape[0]
            if at < total.shape[0]:
                total[at:, :] = jnp.zeros((total.shape[0] - at, total.shape[1]), total.dtype)

    def work(parts):
        deltas = []
        for k in range(3):
            rows = [jnp.where(keep, own[k], got[k]) for own, got in parts]
            deltas.append(rows[0] if len(rows) == 1 else jnp.concatenate(rows, axis=0))
        capped, gate_d, up_d = deltas
        if outs_in:
            total[...] += dot_last(gate_d, gate_w[...]) + dot_last(up_d, up_w[...])
        if do_w:
            gate_g, up_g, down_g = grads
            gate_g[...] = dot_plain(tok_t[...], gate_d).astype(gate_g.dtype)
            up_g[...] = dot_plain(tok_t[...], up_d).astype(up_g.dtype)
            down_g[...] = dot_plain(capped.T, grad[...]).astype(down_g.dtype)

    for low, high, parts in segments:
        if len(segments) == 1:
            work(parts)
        else:
            pl.when((j >= low) & (j < high))(functools.partial(work, parts))

    if outs_in > 1:

        @pl.when(j == pl.num_programs(0) - 1)
        def _():
            at = 0
            for end in ends:
                end[...] = total[at:at + end.shape[0], :]
                at += end.shape[0]


def back(inner, segments, gate_w, up_w, before=(), cuts=(), turned=None, old=None):
    feats, columns = gate_w.shape
    block = pick_block(*(e for s in segments for e in (s[0], s[1], s[3])))
    first = segments[0][0] // block
    rows = sum(own.shape[1] for own, _ in segments[0][2])
    cols = pl.BlockSpec((feats, block), lambda j: (0, first + j))
    in_specs, args, layout, aliases = [pl.BlockSpec(memory_space=pltpu.SMEM)], [inner], [], {}
    at = 0
    for _, width, parts, skip in segments:
        steps = width // block
        layout.append((at, at + steps, len(parts)))
        for own, got in parts:
            in_specs += [within((3, own.shape[1], block), at, steps, skip // block)] * 2
            args += [own, got]
        at += steps
    out_specs, out_shape, scratch = [], [], []
    if cuts:
        in_specs += [cols, cols] + [once(b.shape) for b in before]
        args += [gate_w, up_w, *before]
        out_specs += [pl.BlockSpec((c, feats), lambda j: (0, 0)) for c in cuts]
        out_shape += [jax.ShapeDtypeStruct((c, feats), jnp.float32) for c in cuts]
        if len(cuts) > 1:
            scratch = [pltpu.VMEM((rows, feats), jnp.float32)]
    if turned is not None:
        in_specs += [once(a.shape) for a in turned]
        args += [*turned]
        for k, a in enumerate(old or ()):
            in_specs += [pl.BlockSpec(memory_space=pl.ANY)]
            args += [a]
            aliases[len(args) - 1] = len(cuts) + k
        out_specs += [cols, cols, pl.BlockSpec((block, feats), lambda j: (first + j, 0))]
        out_shape += [jax.ShapeDtypeStruct(s, jnp.bfloat16) for s in ((feats, columns), (feats, columns), (columns, feats))]
    do_w = 0 if turned is None else (2 if old else 1)
    width = at * block
    outs = call(
        functools.partial(back_kernel, tuple(layout), len(before), len(cuts), do_w),
        ("in" if cuts else "") + ("w" if do_w else ""),
        at,
        in_specs,
        out_specs,
        out_shape,
        args,
        aliases,
        scratch,
        flops=((4 if cuts else 0) + (6 if do_w else 0)) * rows * feats * width,
        moved=((4 if cuts else 0) + (6 if do_w else 0)) * feats * width + 8 * rows * feats + 12 * rows * width,
    )
    return outs[:len(cuts)], outs[len(cuts):]


def per_device(n_hid, n_wid, tokens, out_grad, gate_weight, up_weight, down_weight, cap_codes):
    half = n_wid // 2
    chips = n_hid // 2
    columns = gate_weight.shape[1]
    piece = tokens.shape[0] // SLABS
    slab_rows = n_hid * piece
    shared = 4 * BLOCK
    mats = (gate_weight, up_weight, down_weight)

    def across_hid(x, flip):
        return lax.ppermute(x, "hid", [(i, i ^ flip) for i in range(n_hid)])

    def gather(slab, mark):
        rows = slice(slab * piece, (slab + 1) * piece)
        own = jnp.stack([tokens[rows], out_grad[rows]])
        if mark is not None:
            own = tie(own, mark)
        even = [own] + [across_hid(own, 2 * m) for m in range(1, chips)]
        if mark is None:
            return even + [across_hid(part, 1) for part in even]
        both = jnp.concatenate(even, axis=1)
        return [both, across_hid(both, 1)]

    def fold(low, high):
        return (low + across_hid(high, 1)).reshape(chips, -1, low.shape[1])

    def scatter(parts):
        small = jnp.concatenate([p.astype(jnp.bfloat16) for p in parts], axis=1)
        result = jnp.concatenate([p[0] for p in parts], axis=0)
        for m in range(1, chips):
            result = result + across_hid(small[m], 2 * m).astype(jnp.float32)
        return result.astype(jnp.bfloat16)

    codes = cap_codes.reshape(1, -1)
    place = lax.axis_index("wid")
    inner = ((place == half - 1) | (place == half)).astype(jnp.int32).reshape(1)

    units = [(0, shared)] + [(c, min(UNIT, columns - c)) for c in range(shared, columns, UNIT)] + [(0, shared)]
    units[ODD], units[-2] = units[-2], units[ODD]
    count = len(units)
    final = count - 1
    full = list(range(1, final))
    groups = [[u] for u in full]
    fronts = [[u] for u in range(count)]

    sums, message, inward, across, made, got = ({} for _ in range(6))
    mark = None
    panel = None
    held = None
    turned = None

    def run_front(u):
        nonlocal mark, panel, turned, held
        if u in message:
            return
        members = next(b for b in fronts if u in b)
        spans = [units[m] for m in members]
        if u == 0:
            held = gather(0, None)
            panel, outs = front((), held, 0, slab_rows, *mats, spans, inside=True)
        elif u == 1:
            pieces = [*held, *(tie(p, mark) for p in later)]
            panel, outs = front((), pieces, 0, SLABS * slab_rows, *mats, spans)
            turned = (panel[0].T, panel[1])
        else:
            given = (tie(panel[0], mark), panel[1])
            if u == final:
                _, outs = front(given, (), 1, slab_rows, *mats, spans)
            else:
                _, outs = front(given, (), 0, SLABS * slab_rows, *mats, spans)
        for i, m in enumerate(members):
            sums[m], message[m] = outs[2 * i], outs[2 * i + 1]
        mark = message[members[-1]]

    def run_inward(u):
        message[u] = tie(message[u], mark)
        inward[u] = jnp.zeros_like(message[u])
        for k in range(half - 1):
            if k:
                message[u] = (sums[u] + inward[u].astype(jnp.float32)).astype(jnp.bfloat16)
            inward[u] = lax.ppermute(message[u], "wid", [(k, k + 1), (n_wid - 1 - k, n_wid - 2 - k)])

    def send_across(u):
        across[u] = lax.ppermute(message[u], "wid", [(half - 1, half), (half, half - 1)])

    def run_middle(u):
        nonlocal mark
        arrived = tie(inward[u], mark, *(turned[:1] if u == TURN else ()))
        mark = message[u] = (sums[u] + arrived.astype(jnp.float32)).astype(jnp.bfloat16)
        send_across(u)

    def run_hidden(u, joint=False):
        nonlocal mark
        arrived = tie(across[u], mark)
        if joint:
            made[u], message[u + 1] = hidden(sums[u], inward[u], arrived, codes, units[u][0], (sums[u + 1], inward[u + 1]))
            mark = made[u]
            send_across(u + 1)
        else:
            mark = made[u] = hidden(sums[u], inward[u], arrived, codes, units[u][0])
        last = made[u]
        for k in range(half - 1):
            last = lax.ppermute(last, "wid", [(half - 1 - k, half - 2 - k), (half + k, half + k + 1)])
            got[u] = last if k == 0 else got[u] + last

    def pair(u):
        return made[u], got.get(u, made[u])

    total, grads, folded = [], None, []
    rows = SLABS * slab_rows
    quarter = slab_rows // 2

    def run_back(members, cuts, weights):
        nonlocal mark, total, grads
        segments = [(*units[m], [pair(m)], 0) for m in members]
        own, arrived = segments[0][2][0]
        segments[0][2][0] = (own, tie(arrived, mark))
        total, new = back(inner, segments, *mats[:2], before=tuple(total), cuts=cuts, turned=turned if weights else None, old=grads)
        mark = total[-1]
        if weights:
            grads = new

    def run_weights(segments):
        nonlocal mark, grads
        own, arrived = segments[0][2][0]
        segments[0][2][0] = (own, tie(arrived, mark))
        _, grads = back(inner, segments, *mats[:2], turned=turned, old=grads)
        mark = grads[0]

    later = None
    for t in range(-LOOK, count + 1):
        joint = JOINT and t > 0 and t + 2 < count and sums[t].shape == sums[t + 1].shape
        if 0 <= t + 1 < count and not joint:
            run_middle(t + 1)
        if 0 <= t < count:
            run_hidden(t, joint)
        if t + LOOK < count:
            run_front(t + LOOK)
            run_inward(t + LOOK)
            if t + LOOK == 0:
                later = gather(1, mark if HELD < 0 else held[HELD])
        if t > -LOOK:
            for u in range(t + LOOK + 1, min(t + AHEAD + 1, count)):
                run_front(u)
        if t == BACK:
            run_back([0], (slab_rows,), False)
        for g in groups[:-1]:
            if t == g[-1] + BACK:
                run_back(g, (rows,), True)
        if t == groups[-1][-1] + 1:
            run_back(groups[-1], (quarter, quarter, slab_rows), False)
            folded.append(fold(*total[:2]))
            total = total[2:]
        if t == count:
            run_weights([(*units[m], [pair(m)], 0) for m in groups[-1]])
            run_back([final], (quarter, quarter), False)
            folded.append(fold(*total))
            run_weights([(units[0][0], shared, [pair(0), pair(final)], 0)])

    return (scatter(folded), *grads)


def solution(mesh):
    return jax.shard_map(
        functools.partial(per_device, mesh.shape["hid"], mesh.shape["wid"]),
        mesh=mesh,
        in_specs=(
            P("hid", "wid"),
            P("hid", "wid"),
            P("wid", "hid"),
            P("wid", "hid"),
            P("hid", "wid"),
            P("hid"),
        ),
        out_specs=(P("hid", "wid"), P("wid", "hid"), P("wid", "hid"), P("hid", "wid")),
        check_vma=False,
    )
```
